512 devices in a mesh: dp: 32 (over z, core), fsdp: 16 (over y, x).
Axes of the slice: x: 4, y: 4, z: 16, core: 2. Of those that a mesh axis runs over, the one named last changes fastest.
Arguments:
- inputs: bfloat16 [12288, 8192], P('dp', 'fsdp'), may hold values from -6 to 6
- out_grad: bfloat16 [12288, 4096], P('dp', 'fsdp'), may hold values from -6 to 6
- base_weight: bfloat16 [8192, 4096], P('fsdp', 'dp'), may hold values from -0.125 to 0.125
- down_maps: bfloat16 [64, 64, 8192], P('dp', None, 'fsdp'), may hold values from -0.0625 to 0.0625
- up_maps: bfloat16 [64, 64, 4096], P('dp', None, 'fsdp'), may hold values from -0.75 to 0.75
- mean_down: float32 [64, 64, 8192], P('dp', None, 'fsdp'), may hold values from -0.5 to 0.5
- square_down: float32 [64, 64, 8192], P('dp', None, 'fsdp'), may hold values from 0.25 to 1.25
- mean_up: float32 [64, 64, 4096], P('dp', None, 'fsdp'), may hold values from -0.5 to 0.5
- square_up: float32 [64, 64, 4096], P('dp', None, 'fsdp'), may hold values from 0.25 to 1.25
- block_member: int32 [1536], P('dp'), may hold values from 0 to 63, as said below
- member_slot: int32 [64], replicated, may hold values from 0 to 63, as said below
Outputs:
- projected: bfloat16 [12288, 4096], P('dp', 'fsdp')
- new_mean_down: float32 [64, 64, 8192], P('dp', None, 'fsdp')
- new_square_down: float32 [64, 64, 8192], P('dp', None, 'fsdp')
- new_mean_up: float32 [64, 64, 4096], P('dp', None, 'fsdp')
- new_square_up: float32 [64, 64, 4096], P('dp', None, 'fsdp')
The draws below stay inside these ranges and needn't reach their ends.
Inputs may be any that keep to these rules, and one draw needn't show every extreme that they name: `block_member`: of the 48 blocks of one dp index, at most 3 have members whose slots lie with one dp index; in every draw some dp index receives exactly 3 blocks from every dp index. `member_slot`: A permutation: every slot once. Slot s lies with dp index s // 2.
All inputs are finite; a program needn't handle non-finite values.
Results may differ from the reference program's by a relative error of at most 0.022.
Values may be sent and summed in bfloat16 or wider, within the bound.
A program may use at most 64 MiB of HBM per device.

```python
import jax
import jax.numpy as jnp
from jax import lax

D = 8192
DOUT = 4096
RANK = 64
MEM_DEV = 2
BLK = 8
SNAPS = 2
MEMBERS = 64
BLOCKS = 48
CAP = 3
ALL_ROWS = 12288
BLOCKS_ALL = 1536
N_DP = 32
N_FSDP = 16


def slot_table(key):
    return jax.random.permutation(jax.random.fold_in(key, 11), MEMBERS).astype(jnp.int32)


def draw_member_slot(key, part):
    return slot_table(key)


def draw_block_member(key, part):
    slots = slot_table(key)
    slot_member = jnp.zeros((MEMBERS,), jnp.int32).at[slots].set(jnp.arange(MEMBERS, dtype=jnp.int32))
    busiest = jax.random.randint(jax.random.fold_in(key, 12), (), 0, N_DP).astype(jnp.int32)

    def one_index(index_key):
        first_key, second_key, third_key = jax.random.split(index_key, 3)
        others = jax.random.permutation(first_key, (N_DP - 1) * CAP)[:BLOCKS - CAP].astype(jnp.int32)
        owners = (others // CAP + busiest + 1) % N_DP
        owners = jnp.concatenate([jnp.full((CAP,), busiest, jnp.int32), owners])
        owners = owners[jax.random.permutation(second_key, BLOCKS)]
        within = jax.random.randint(third_key, (BLOCKS,), 0, MEM_DEV).astype(jnp.int32)
        return slot_member[owners * MEM_DEV + within]
    index_keys = jax.random.split(jax.random.fold_in(key, 13), N_DP)
    return jax.vmap(one_index)(index_keys).reshape(-1).astype(jnp.int32)


def with_spikes(entries, rng, source, target, shards_of, factor):
    def block_of(axis_at):
        return (jnp.arange(entries.shape[axis_at]) // (entries.shape[axis_at] // shards_of)).reshape((-1,) + (1,) * (entries.ndim - 1 - axis_at))

    one_side = jax.random.permutation(rng, shards_of)[block_of(target)]
    other_side = (block_of(target) + shards_of // 2) % shards_of
    return jnp.where((block_of(source) == one_side) | (block_of(source) == other_side), factor * entries, entries)


def level_of(own_key, dims, cuts, least, high):
    def one(dim, blocks):
        steps = jax.random.uniform(jax.random.fold_in(jax.random.fold_in(own_key, 6), dim), (blocks,), jnp.float32, least / len(cuts), high / len(cuts))
        return jnp.repeat(jnp.exp(steps), dims[dim] // blocks).reshape((-1,) + (1,) * (len(dims) - dim - 1))

    loudness = one(*cuts[0])
    for cut in cuts[1:]:
        loudness = loudness * one(*cut)
    return loudness


def normal_values(own_key, extent, spread, bound, shards=(), held_as=jnp.bfloat16):
    result = spread * jax.random.normal(own_key, extent, jnp.float32)
    if shards:
        result = result * level_of(own_key, extent, shards, -0.22, 0.18)
    return jnp.clip(result, -bound, bound).astype(held_as)


def noise_with(own_key, shape, width, bound, pieces, heavy, kind=jnp.bfloat16):
    result = width * jax.random.normal(own_key, shape, jnp.float32)
    if pieces:
        result = result * level_of(own_key, shape, pieces, -0.22, 0.18)
    return jnp.clip(with_spikes(result, jax.random.fold_in(own_key, 3), *heavy), -bound, bound).astype(kind)


def setup_inputs(seed: int = 0) -> dict:
    seeds = jax.random.split(jax.random.key(seed), 12)
    return {
        "inputs": normal_values(seeds[0], (ALL_ROWS, D), 1.0, 6.0, ((0, 32), (1, 16))),
        "out_grad": normal_values(seeds[1], (ALL_ROWS, DOUT), 1.0, 6.0, ((0, 32), (1, 16))),
        "base_weight": noise_with(seeds[2], (D, DOUT), D ** -0.5, 0.125, ((0, 16), (1, 32)), (0, 1, 32, 2.75)),
        "down_maps": normal_values(seeds[3], (MEMBERS, RANK, D), D ** -0.5, 0.0625, ((0, 32), (2, 16))),
        "up_maps": normal_values(seeds[4], (MEMBERS, RANK, DOUT), RANK ** -0.5, 0.75, ((0, 32), (2, 16))),
        "mean_down": normal_values(seeds[5], (MEMBERS, RANK, D), 0.2, 0.5, ((0, 32), (2, 16)), jnp.float32),
        "square_down": jnp.clip(0.25 + 1.0 * jax.random.uniform(seeds[6], (MEMBERS, RANK, D), jnp.float32) ** level_of(seeds[6], (MEMBERS, RANK, D), ((0, 32), (2, 16)), -0.2, 0.2), 0.25, 1.25),
        "mean_up": normal_values(seeds[7], (MEMBERS, RANK, DOUT), 0.2, 0.5, ((0, 32), (2, 16)), jnp.float32),
        "square_up": jnp.clip(0.25 + 1.0 * jax.random.uniform(seeds[8], (MEMBERS, RANK, DOUT), jnp.float32) ** level_of(seeds[8], (MEMBERS, RANK, DOUT), ((0, 32), (2, 16)), -0.2, 0.2), 0.25, 1.25),
        "block_member": draw_block_member(jax.random.fold_in(seeds[11], 71), 0),
        "member_slot": draw_member_slot(jax.random.fold_in(seeds[11], 71), 0),
    }


adapter_scale = 2.0
rate_down = 0.002
rate_up = 0.02
contract_last = (((1,), (1,)), ((), ()))


def reference(inputs, out_grad, base_weight, down_maps, up_maps, mean_down, square_down, mean_up, square_up, block_member, member_slot):
    slab_width = D // N_FSDP
    input_slabs = inputs.reshape(ALL_ROWS, N_FSDP, slab_width).transpose(1, 0, 2)
    weight_slabs = base_weight.reshape(N_FSDP, slab_width, DOUT)

    def add_slab(running, operands):
        product = jnp.dot(operands[0], operands[1], preferred_element_type=jnp.float32)
        product = lax.optimization_barrier(product.astype(jnp.bfloat16))
        return running + product.astype(jnp.float32), None

    base_sum, _ = lax.scan(add_slab, jnp.zeros((ALL_ROWS, DOUT), jnp.float32), (input_slabs, weight_slabs))
    block_slot = member_slot[block_member].astype(jnp.int32)
    input_blocks = inputs.reshape(BLOCKS_ALL, BLK, D)
    grad_blocks = out_grad.reshape(BLOCKS_ALL, BLK, DOUT)

    def one_block(gradients, operands):
        down_gradient, up_gradient = gradients
        input_block_rows, gradient_block_rows, member_slot_index = operands
        down_map = lax.dynamic_index_in_dim(down_maps, member_slot_index, 0, keepdims=False)
        up_projection_weight = lax.dynamic_index_in_dim(up_maps, member_slot_index, 0, keepdims=False)
        low_rank_product = lax.dot_general(input_block_rows, down_map, contract_last, preferred_element_type=jnp.float32).astype(jnp.bfloat16)
        backward_low_rank = lax.dot_general(gradient_block_rows, up_projection_weight, contract_last, preferred_element_type=jnp.float32).astype(jnp.bfloat16)
        adapted_output = (adapter_scale * jnp.dot(low_rank_product, up_projection_weight, preferred_element_type=jnp.float32)).astype(jnp.bfloat16)
        down_gradient = down_gradient.at[member_slot_index].add(adapter_scale * jnp.dot(backward_low_rank.T, input_block_rows, preferred_element_type=jnp.float32))
        up_gradient = up_gradient.at[member_slot_index].add(adapter_scale * jnp.dot(low_rank_product.T, gradient_block_rows, preferred_element_type=jnp.float32))
        return (down_gradient, up_gradient), adapted_output

    zeros_down = jnp.zeros((MEMBERS, RANK, D), jnp.float32)
    zeros_up = jnp.zeros((MEMBERS, RANK, DOUT), jnp.float32)
    (down_gradient, up_gradient), adapted_output = lax.scan(one_block, (zeros_down, zeros_up), (input_blocks, grad_blocks, block_slot))
    projected = (base_sum + adapted_output.reshape(ALL_ROWS, DOUT).astype(jnp.float32)).astype(jnp.bfloat16)
    theta_down = down_maps.astype(jnp.float32) - rate_down * down_gradient
    theta_up = up_maps.astype(jnp.float32) - rate_up * up_gradient
    denominator = SNAPS + 1.0
    new_mean_down = (SNAPS * mean_down + theta_down) / denominator
    new_square_down = (SNAPS * square_down + theta_down * theta_down) / denominator
    new_mean_up = (SNAPS * mean_up + theta_up) / denominator
    new_square_up = (SNAPS * square_up + theta_up * theta_up) / denominator
    return (projected, new_mean_down, new_square_down, new_mean_up, new_square_up)
```

```python
import functools

import jax
import jax.numpy as jnp
from jax import lax
from jax.experimental import pallas as pl
from jax.experimental.pallas import tpu as pltpu
from jax.sharding import PartitionSpec as P

SNAPS = 2
BLK = 8

adapter_scale = 2.0
rate_down = 0.002
rate_up = 0.02
contract_last = (((1,), (1,)), ((), ()))
contract_first = (((0,), (0,)), ((), ()))
MESH = pl.DeviceIdType.MESH
GROUP = 4

f32 = jnp.float32
bf16 = jnp.bfloat16


def iota(shape, dim):
    return lax.broadcasted_iota(jnp.int32, shape, dim)


def to_column(row):
    n = row.shape[1]
    return jnp.sum(jnp.where(iota((n, n), 0) == iota((n, n), 1), row, 0), axis=1, keepdims=True)


def kernel(
    sizes,
    x_ref, g_ref, w_ref, d_ref, u_ref, member_ref, slot_ref,
    out_ref, gd_ref, gu_ref,
    w_all, disp_send, disp_recv, tag_send, tag_recv,
    part_send, part_recv, lr_send, lr_recv, lr_all, ret_send, ret_recv, acc,
    ring_r_send, ring_r_recv, ring_l_send, ring_l_recv, sib_send, sib_recv,
    disp_ssem, disp_rsem, tag_ssem, tag_rsem, part_ssem, part_rsem,
    rs_ssem, rs_rsem, ag_ssem, ag_rsem, ret_ssem, ret_rsem,
):
    n_dp, n_f, cap = sizes
    n_z = n_dp // 2
    half_z = n_z // 2
    rows, slab = x_ref.shape
    width = g_ref.shape[1]
    hs, hw = slab // 2, width // 2
    blocks = member_ref.shape[1]
    members = slot_ref.shape[1]
    chunk = cap * BLK
    me = lax.axis_index("dp")
    fs = lax.axis_index("fsdp")
    z, core = me // 2, me % 2
    right = lax.rem(z + 1, n_z) * 2 + core
    left = lax.rem(z + n_z - 1, n_z) * 2 + core
    sibling = z * 2 + (1 - core)

    def dp_copy(src, dst, send_sem, recv_sem, to):
        return pltpu.make_async_remote_copy(
            src_ref=src, dst_ref=dst, send_sem=send_sem, recv_sem=recv_sem,
            device_id=(to, fs), device_id_type=MESH,
        )

    def f_copy(src, dst, send_sem, recv_sem, to):
        return pltpu.make_async_remote_copy(
            src_ref=src, dst_ref=dst, send_sem=send_sem, recv_sem=recv_sem,
            device_id=(me, to), device_id_type=MESH,
        )

    barrier = pltpu.get_barrier_semaphore()

    @pl.loop(1, n_dp)
    def _(k):
        pl.semaphore_signal(barrier, inc=1, device_id=(lax.rem(me + k, n_dp), fs), device_id_type=MESH)

    @pl.loop(1, n_f)
    def _(k):
        pl.semaphore_signal(barrier, inc=1, device_id=(me, lax.rem(fs + k, n_f)), device_id_type=MESH)

    slot_col = to_column(slot_ref[...])
    slots = jnp.sum(
        jnp.where(iota((members, blocks), 0) == member_ref[...], slot_col, 0), axis=0, keepdims=True
    )
    owner = slots // 2
    local = slots - owner * 2
    owner_col = to_column(owner)
    earlier = (owner_col == owner) & (iota((blocks, blocks), 0) < iota((blocks, blocks), 1))
    position = jnp.sum(jnp.where(earlier, 1, 0), axis=0, keepdims=True)
    target = owner * cap + position
    target_col = to_column(target)
    local_col = to_column(local)
    row_target = (
        jnp.sum(
            jnp.where(iota((blocks, rows), 0) == iota((blocks, rows), 1) // BLK, target_col, 0),
            axis=0, keepdims=True,
        ) * BLK
        + iota((1, rows), 1) % BLK
    )
    row_target_col = (
        jnp.sum(
            jnp.where(iota((rows, blocks), 1) == iota((rows, blocks), 0) // BLK, target, 0),
            axis=1, keepdims=True,
        ) * BLK
        + iota((rows, 1), 0) % BLK
    )
    tag_send[0] = jnp.sum(
        jnp.where(target_col == iota((blocks, 128), 1), local_col, 0), axis=0, keepdims=True
    )
    tag_recv[pl.ds(me, 1)] = tag_send[...]
    w_all[pl.ds(z, 1), pl.ds(core, 1)] = w_ref[...].reshape(1, 1, *w_ref.shape)

    halves = [
        jnp.concatenate([x_ref[:, h * hs:(h + 1) * hs], g_ref[:, h * hw:(h + 1) * hw]], axis=1)
        for h in range(2)
    ]

    @pl.loop(0, n_dp // GROUP)
    def _(i):
        pick = jnp.where(
            iota((GROUP * chunk, rows), 0) + i * (GROUP * chunk) == row_target, 1.0, 0.0
        ).astype(bf16)
        both = [
            jnp.dot(pick, half, preferred_element_type=f32).reshape(GROUP, chunk, hs + hw)
            for half in halves
        ]
        disp_send[pl.ds(i * GROUP, GROUP)] = jnp.concatenate(both, axis=1).astype(bf16)

    disp_recv[pl.ds(me, 1)] = disp_send[pl.ds(me, 1)]

    pl.semaphore_wait(barrier, n_dp + n_f - 2)

    def ring_right(src_z, step):
        block = w_all.at[src_z, core]
        return dp_copy(block, block, ring_r_send.at[step], ring_r_recv.at[step], right)

    def ring_left(src_z, step):
        block = w_all.at[src_z, core]
        return dp_copy(block, block, ring_l_send.at[step], ring_l_recv.at[step], left)

    def to_sibling(src_z):
        block = w_all.at[src_z, core]
        return dp_copy(block, block, sib_send.at[src_z], sib_recv.at[src_z], sibling)

    def from_sibling(src_z):
        block = w_all.at[src_z, 1 - core]
        return dp_copy(block, block, sib_send.at[src_z], sib_recv.at[src_z], sibling)

    def start_ring():
        ring_right(z, 1).start()
        ring_left(z, 1).start()
        to_sibling(z).start()

    def disp_to(k):
        to = lax.rem(me + k, n_dp)
        return dp_copy(disp_send.at[to], disp_recv.at[me], disp_ssem.at[to], disp_rsem.at[me], to)

    def disp_from(p):
        return dp_copy(disp_send.at[p], disp_recv.at[p], disp_ssem.at[p], disp_rsem.at[p], p)

    def tag_to(k):
        to = lax.rem(me + k, n_dp)
        return dp_copy(tag_send.at[0], tag_recv.at[me], tag_ssem.at[to], tag_rsem.at[me], to)

    def tag_from(p):
        return dp_copy(tag_send.at[0], tag_recv.at[p], tag_ssem.at[p], tag_rsem.at[p], p)

    start_ring()

    @pl.loop(1, n_dp)
    def _(k):
        tag_to(k).start()
        disp_to(k).start()

    def part_to(j):
        return f_copy(part_send.at[j], part_recv.at[fs], part_ssem.at[j], part_rsem.at[fs], j)

    def part_from(j):
        return f_copy(part_send.at[j], part_recv.at[j], part_ssem.at[j], part_rsem.at[j], j)

    def term(j):
        from_sibling(j).wait_recv()
        part_send[pl.ds(j, 1)] = jnp.concatenate(
            [jnp.dot(x_ref[...], w_all[j, c], preferred_element_type=f32) for c in range(2)], axis=1
        ).astype(bf16)[None]

        @pl.when(j == fs)
        def _():
            part_recv[pl.ds(j, 1)] = part_send[pl.ds(j, 1)]

        @pl.when(j != fs)
        def _():
            part_to(j).start()

    def from_left(step):
        return lax.rem(z + n_z - step, n_z)

    def from_right(step):
        return lax.rem(z + step, n_z)

    term(z)

    @pl.loop(1, half_z)
    def _(s):
        ring_right(from_left(s), s).wait_recv()
        ring_right(from_left(s), s + 1).start()
        to_sibling(from_left(s)).start()
        ring_left(from_right(s), s).wait_recv()

        @pl.when(s < half_z - 1)
        def _():
            ring_left(from_right(s), s + 1).start()
        to_sibling(from_right(s)).start()

        @pl.when(s > 1)
        def _():
            @pl.loop(0, 2)
            def _(k):
                term(lax.rem(z + n_z + (s - 1) * (2 * k - 1), n_z))

    ring_right(from_left(half_z), half_z).wait_recv()
    to_sibling(from_left(half_z)).start()

    @pl.loop(0, 3)
    def _(k):
        term(lax.rem(z + n_z + jnp.where(k == 0, 1 - half_z, half_z - 2 + k), n_z))

    @pl.loop(1, n_dp)
    def _(k):
        p = lax.rem(me + n_dp - k, n_dp)
        tag_from(p).wait_recv()
        disp_from(p).wait_recv()

    first = iota((GROUP * chunk, 128), 1) < 64

    def tags_of(i):
        tags = tag_recv[pl.ds(i * GROUP, GROUP)]
        shape = (GROUP, chunk, 128)
        mine = iota(shape, 2) == me * cap + iota(shape, 1) // BLK
        tag = jnp.sum(jnp.where(mine, tags.astype(f32), 0.0), axis=2, keepdims=True)
        return jnp.broadcast_to(tag, shape).reshape(GROUP * chunk, 128) > 0.5

    def fold(value):
        value = value.reshape(GROUP, 2 * chunk, value.shape[1])
        return value[:, :chunk], value[:, chunk:]

    def projected(got, maps, half):
        one = lax.dot_general(got, maps[:, :half], contract_last, preferred_element_type=f32)
        two = lax.dot_general(got, maps[:, half:], contract_last, preferred_element_type=f32)
        return (fold(one)[0] + fold(two)[1]).reshape(GROUP * chunk, 128)

    @pl.loop(0, n_dp // GROUP)
    def _(i):
        got = disp_recv[pl.ds(i * GROUP, GROUP)].reshape(GROUP * 2 * chunk, hs + hw)
        low = projected(got[:, :hs], d_ref[...], hs)
        back = projected(got[:, hs:], u_ref[...], hw)
        tag = tags_of(i)
        low = jnp.where(tag, pltpu.roll(low, 64, 1), low)
        back = jnp.where(tag, back, pltpu.roll(back, 64, 1))
        lr_send[pl.ds(i * 2, 2)] = jnp.where(first, low, back).reshape(2, 2 * chunk, 128).astype(bf16)

    lr_recv[pl.ds(fs, 1)] = lr_send[pl.ds(fs, 1)]

    def rs_to(j):
        return f_copy(lr_send.at[j], lr_recv.at[fs], rs_ssem.at[j], rs_rsem.at[fs], j)

    def rs_from(j):
        return f_copy(lr_send.at[j], lr_recv.at[j], rs_ssem.at[j], rs_rsem.at[j], j)

    def ag_to(j):
        return f_copy(lr_all.at[fs], lr_all.at[fs], ag_ssem.at[j], ag_rsem.at[fs], j)

    def ag_from(j):
        return f_copy(lr_all.at[j], lr_all.at[j], ag_ssem.at[j], ag_rsem.at[j], j)

    def others(n, mine, act):
        @pl.loop(1, n)
        def _(k):
            act(lax.rem(mine + k, n))

    others(n_f, fs, lambda j: rs_to(j).start())
    others(n_f, fs, lambda j: rs_from(j).wait_recv())
    lr_all[pl.ds(fs, 1)] = jnp.sum(lr_recv[...].astype(f32), axis=0).astype(bf16)[None]
    others(n_f, fs, lambda j: ag_to(j).start())
    others(n_f, fs, lambda j: ag_from(j).wait_recv())

    def spread(i):
        value = lr_all[pl.ds(i * 2, 2)].reshape(GROUP * chunk, 128).astype(f32)
        turned = pltpu.roll(value, 64, 1)
        tag = tags_of(i)
        low = jnp.where(first, jnp.where(tag, 0.0, value), jnp.where(tag, turned, 0.0))
        back = jnp.where(first, jnp.where(tag, 0.0, turned), jnp.where(tag, value, 0.0))
        return low, back

    @pl.loop(0, n_dp // GROUP)
    def _(i):
        low, _ = spread(i)
        adapted = adapter_scale * jnp.dot(low.astype(bf16), u_ref[...], preferred_element_type=f32)
        adapted = adapted.reshape(GROUP, chunk, width)
        ret_send[pl.ds(i * GROUP, GROUP)] = jnp.concatenate(
            [adapted[:, :, :hw], adapted[:, :, hw:]], axis=1
        ).astype(bf16)

    def ret_to(p):
        return dp_copy(ret_send.at[p], ret_recv.at[me], ret_ssem.at[p], ret_rsem.at[me], p)

    def ret_from(p):
        return dp_copy(ret_send.at[p], ret_recv.at[p], ret_ssem.at[p], ret_rsem.at[p], p)

    others(n_dp, me, lambda p: ret_to(p).start())
    ret_recv[pl.ds(me, 1)] = ret_send[pl.ds(me, 1)]

    gd_ref[...] = jnp.zeros_like(gd_ref)
    gu_ref[...] = jnp.zeros_like(gu_ref)

    @pl.loop(0, n_dp // GROUP)
    def _(i):
        got = disp_recv[pl.ds(i * GROUP, GROUP)].reshape(GROUP * 2 * chunk, hs + hw)
        low, back = spread(i)
        low = low.reshape(GROUP, chunk, 128)
        back = back.reshape(GROUP, chunk, 128)
        zero = jnp.zeros_like(low)

        def part(value, h, rows_of):
            pair = [value, zero] if h == 0 else [zero, value]
            wide = jnp.concatenate(pair, axis=1).reshape(GROUP * 2 * chunk, 128).astype(bf16)
            return lax.dot_general(wide, rows_of, contract_first, preferred_element_type=f32)

        for h in range(2):
            gd_ref[:, h * hs:(h + 1) * hs] += part(back, h, got[:, :hs])
            gu_ref[:, h * hw:(h + 1) * hw] += part(low, h, got[:, hs:])

    others(n_f, fs, lambda j: part_from(j).wait_recv())
    acc[...] = part_recv[0].astype(f32)

    @pl.loop(1, n_f)
    def _(j):
        acc[...] += part_recv[j].astype(f32)

    others(n_dp, me, lambda p: ret_from(p).wait_recv())

    @pl.loop(0, n_dp // GROUP)
    def _(i):
        one, two = fold(
            ret_recv[pl.ds(i * GROUP, GROUP)].astype(f32).reshape(GROUP * 2 * chunk, hw)
        )
        value = jnp.concatenate([one, two], axis=2).reshape(GROUP * chunk, width).astype(bf16)
        pick = jnp.where(
            iota((rows, GROUP * chunk), 1) + i * (GROUP * chunk) == row_target_col, 1.0, 0.0
        ).astype(bf16)
        acc[...] += jnp.dot(pick, value, preferred_element_type=f32)

    out_ref[...] = acc[...].astype(bf16)

    ring_right(z, 1).wait_send()
    ring_left(z, 1).wait_send()
    to_sibling(z).wait_send()

    @pl.loop(1, half_z)
    def _(s):
        ring_right(from_left(s), s + 1).wait_send()
        to_sibling(from_left(s)).wait_send()

        @pl.when(s < half_z - 1)
        def _():
            ring_left(from_right(s), s + 1).wait_send()
        to_sibling(from_right(s)).wait_send()

    to_sibling(from_left(half_z)).wait_send()

    @pl.loop(1, n_dp)
    def _(k):
        tag_to(k).wait_send()
        disp_to(k).wait_send()
        ret_to(lax.rem(me + k, n_dp)).wait_send()

    @pl.loop(1, n_f)
    def _(k):
        j = lax.rem(fs + k, n_f)
        part_to(j).wait_send()
        rs_to(j).wait_send()
        ag_to(j).wait_send()


def fused(x, g, w, down, up, block_member, member_slot):
    n_dp, n_f = lax.axis_size("dp"), lax.axis_size("fsdp")
    rows, slab = x.shape
    width = g.shape[1]
    cap = 2 * block_member.shape[1] // n_dp
    chunk = cap * BLK
    n_z = n_dp // 2
    vmem = pl.BlockSpec(memory_space=pltpu.VMEM)
    dma = pltpu.SemaphoreType.DMA
    return pl.pallas_call(
        functools.partial(kernel, (n_dp, n_f, cap)),
        out_shape=(
            jax.ShapeDtypeStruct((rows, width), bf16),
            jax.ShapeDtypeStruct(down.shape, f32),
            jax.ShapeDtypeStruct(up.shape, f32),
        ),
        in_specs=[vmem] * 7,
        out_specs=(vmem,) * 3,
        scratch_shapes=[
            pltpu.VMEM((n_z, 2, *w.shape), bf16),
            pltpu.VMEM((n_dp, 2 * chunk, (slab + width) // 2), bf16),
            pltpu.VMEM((n_dp, 2 * chunk, (slab + width) // 2), bf16),
            pltpu.VMEM((1, 1, 128), jnp.int32),
            pltpu.VMEM((n_dp, 1, 128), jnp.int32),
            pltpu.VMEM((n_f, rows, width), bf16),
            pltpu.VMEM((n_f, rows, width), bf16),
            pltpu.VMEM((n_f, 2 * chunk, 128), bf16),
            pltpu.VMEM((n_f, 2 * chunk, 128), bf16),
            pltpu.VMEM((n_f, 2 * chunk, 128), bf16),
            pltpu.VMEM((n_dp, 2 * chunk, width // 2), bf16),
            pltpu.VMEM((n_dp, 2 * chunk, width // 2), bf16),
            pltpu.VMEM((rows, width), f32),
            dma((n_z // 2 + 1,)), dma((n_z // 2 + 1,)), dma((n_z // 2 + 1,)), dma((n_z // 2 + 1,)),
            dma((n_z,)), dma((n_z,)),
            dma((n_dp,)), dma((n_dp,)), dma((n_dp,)), dma((n_dp,)),
            dma((n_f,)), dma((n_f,)), dma((n_f,)), dma((n_f,)), dma((n_f,)), dma((n_f,)),
            dma((n_dp,)), dma((n_dp,)),
        ],
        compiler_params=pltpu.CompilerParams(
            collective_id=0, has_side_effects=True, vmem_limit_bytes=40 * 1024 * 1024
        ),
        name="adapter_step",
    )(x, g, w, down, up, block_member, member_slot)


def body(
    inputs, out_grad, base_weight, down_maps, up_maps,
    mean_down, square_down, mean_up, square_up, block_member, member_slot,
):
    owned, rank, slab_width = down_maps.shape
    out_width = up_maps.shape[2]
    projected, down_gradient, up_gradient = fused(
        inputs,
        out_grad,
        base_weight,
        down_maps.reshape(owned * rank, slab_width),
        up_maps.reshape(owned * rank, out_width),
        block_member.reshape(1, -1),
        member_slot.reshape(1, -1),
    )
    theta_down = down_maps.astype(f32) - (rate_down * adapter_scale) * down_gradient.reshape(down_maps.shape)
    theta_up = up_maps.astype(f32) - (rate_up * adapter_scale) * up_gradient.reshape(up_maps.shape)
    denominator = SNAPS + 1.0
    new_mean_down = (SNAPS * mean_down + theta_down) / denominator
    new_square_down = (SNAPS * square_down + theta_down * theta_down) / denominator
    new_mean_up = (SNAPS * mean_up + theta_up) / denominator
    new_square_up = (SNAPS * square_up + theta_up * theta_up) / denominator
    return (projected, new_mean_down, new_square_down, new_mean_up, new_square_up)


def solution(mesh):
    split = P("dp", None, "fsdp")
    placed = (P("dp", "fsdp"), P("dp", "fsdp"), P("fsdp", "dp")) + (split,) * 6 + (P("dp"), P())
    return jax.shard_map(
        body,
        mesh=mesh,
        in_specs=placed,
        out_specs=(P("dp", "fsdp"),) + (split,) * 4,
        check_vma=False,
    )
```

```python
import functools

import jax
import jax.numpy as jnp
from jax import lax
from jax.experimental import pallas as pl
from jax.experimental.pallas import tpu as pltpu
from jax.sharding import PartitionSpec as P

SNAPS = 2
BLK = 8

adapter_scale = 2.0
rate_down = 0.002
rate_up = 0.02
contract_last = (((1,), (1,)), ((), ()))
contract_first = (((0,), (0,)), ((), ()))
MESH = pl.DeviceIdType.MESH
GROUP = 4
PIECES = 3

f32 = jnp.float32
bf16 = jnp.bfloat16


def iota(shape, dim):
    return lax.broadcasted_iota(jnp.int32, shape, dim)


def to_column(row):
    n = row.shape[1]
    return jnp.sum(jnp.where(iota((n, n), 0) == iota((n, n), 1), row, 0), axis=1, keepdims=True)


def kernel(
    sizes,
    x_hbm, g_hbm, w_hbm, d_hbm, u_hbm, member_ref, slot_ref,
    out_ref, gd_ref, gu_ref,
    x_ref, g_ref, d_ref, u_ref, wt_all, disp_send, disp_recv,
    part_send, part_recv, lr_send, lr_recv, lr_all, ret_send, ret_recv, acc,
    in_sem, ring_r_send, ring_r_recv, ring_l_send, ring_l_recv, sib_send, sib_recv,
    disp_ssem, disp_rsem, part_ssem, part_rsem,
    rs_ssem, rs_rsem, ag_ssem, ag_rsem, ret_ssem, ret_rsem,
):
    n_dp, n_f, cap = sizes
    n_z = n_dp // 2
    half_z = n_z // 2
    rows, slab = x_hbm.shape
    width = g_hbm.shape[1]
    hs, hw = slab // 2, width // 2
    blocks = member_ref.shape[1]
    members = slot_ref.shape[1]
    chunk = cap * BLK
    depth = w_hbm.shape[0]
    me = lax.axis_index("dp")
    fs = lax.axis_index("fsdp")
    z, core = me // 2, me % 2
    right = lax.rem(z + 1, n_z) * 2 + core
    left = lax.rem(z + n_z - 1, n_z) * 2 + core
    sibling = z * 2 + (1 - core)
    last = n_dp - 2 + core

    def offset(m):
        return jnp.where(m % 2 == 1, half_z - (m + 1) // 2, m // 2 + n_z - half_z)

    def receiver(i):
        return lax.rem(z + offset(i // 2), n_z) * 2 + i % 2

    def sender(i):
        return lax.rem(z + n_z - lax.rem(offset(i // 2), n_z), n_z) * 2 + i % 2

    def places(start, stop, act):
        @pl.loop(start, stop)
        def _(i):
            @pl.when(i != last)
            def _():
                act(i)

    def dp_copy(src, dst, send_sem, recv_sem, to):
        return pltpu.make_async_remote_copy(
            src_ref=src, dst_ref=dst, send_sem=send_sem, recv_sem=recv_sem,
            device_id=(to, fs), device_id_type=MESH,
        )

    def f_copy(src, dst, send_sem, recv_sem, to):
        return pltpu.make_async_remote_copy(
            src_ref=src, dst_ref=dst, send_sem=send_sem, recv_sem=recv_sem,
            device_id=(me, to), device_id_type=MESH,
        )

    barrier = pltpu.get_barrier_semaphore()
    loads = [
        pltpu.make_async_copy(src, dst, in_sem.at[i])
        for i, (src, dst) in enumerate(
            [(x_hbm, x_ref), (g_hbm, g_ref), (w_hbm, wt_all.at[z, core, pl.ds(0, depth)]), (d_hbm, d_ref), (u_hbm, u_ref)]
        )
    ]
    for load in loads:
        load.start()

    @pl.loop(1, n_dp)
    def _(k):
        pl.semaphore_signal(barrier, inc=1, device_id=(lax.rem(me + k, n_dp), fs), device_id_type=MESH)

    @pl.loop(1, n_f)
    def _(k):
        pl.semaphore_signal(barrier, inc=1, device_id=(me, lax.rem(fs + k, n_f)), device_id_type=MESH)

    slot_col = to_column(slot_ref[...])
    slots = jnp.sum(
        jnp.where(iota((members, blocks), 0) == member_ref[...], slot_col, 0), axis=0, keepdims=True
    )
    owner = slots // 2
    local = slots - owner * 2
    owner_col = to_column(owner)
    earlier = (owner_col == owner) & (iota((blocks, blocks), 0) < iota((blocks, blocks), 1))
    position = jnp.sum(jnp.where(earlier, 1, 0), axis=0, keepdims=True)
    target = owner * cap + position
    target_col = to_column(target)
    local_col = to_column(local)
    row_target = (
        jnp.sum(
            jnp.where(iota((blocks, rows), 0) == iota((blocks, rows), 1) // BLK, target_col, 0),
            axis=0, keepdims=True,
        ) * BLK
        + iota((1, rows), 1) % BLK
    )
    row_target_col = (
        jnp.sum(
            jnp.where(iota((rows, blocks), 1) == iota((rows, blocks), 0) // BLK, target, 0),
            axis=1, keepdims=True,
        ) * BLK
        + iota((rows, 1), 0) % BLK
    )
    tags = jnp.sum(
        jnp.where(target_col == iota((blocks, 128), 1), local_col, 0), axis=0, keepdims=True
    )
    wt_all[pl.ds(z, 1), pl.ds(core, 1), pl.ds(depth, 16)] = jnp.broadcast_to(
        tags.astype(f32), (16, 128)
    ).astype(bf16)[None, None]
    for load in loads:
        load.wait()

    halves = [
        jnp.concatenate([x_ref[:, h * hs:(h + 1) * hs], g_ref[:, h * hw:(h + 1) * hw]], axis=1)
        for h in range(2)
    ]

    @pl.loop(0, n_dp // GROUP)
    def _(i):
        pick = jnp.where(
            iota((GROUP * chunk, rows), 0) + i * (GROUP * chunk) == row_target, 1.0, 0.0
        ).astype(bf16)
        both = [
            jnp.dot(pick, half, preferred_element_type=f32).reshape(GROUP, chunk, hs + hw)
            for half in halves
        ]
        disp_send[pl.ds(i * GROUP, GROUP)] = jnp.concatenate(both, axis=1).astype(bf16)

    disp_recv[pl.ds(last, 1)] = disp_send[pl.ds(me, 1)]

    pl.semaphore_wait(barrier, n_dp + n_f - 2)

    piece = wt_all.shape[2] // PIECES

    def ring_right(src_z, step, q):
        block = wt_all.at[src_z, core, pl.ds(pl.multiple_of(q * piece, piece), piece)]
        at = step * PIECES + q
        return dp_copy(block, block, ring_r_send, ring_r_recv.at[at], right)

    def ring_left(src_z, step, q):
        block = wt_all.at[src_z, core, pl.ds(pl.multiple_of(q * piece, piece), piece)]
        at = step * PIECES + q
        return dp_copy(block, block, ring_l_send, ring_l_recv.at[at], left)

    def to_sibling(src_z):
        block = wt_all.at[src_z, core]
        return dp_copy(block, block, sib_send, sib_recv.at[src_z], sibling)

    def from_sibling(src_z):
        block = wt_all.at[src_z, 1 - core]
        return dp_copy(block, block, sib_send, sib_recv.at[src_z], sibling)

    def start_ring():
        @pl.loop(0, PIECES)
        def _(q):
            ring_right(z, 1, q).start()
            ring_left(z, 1, q).start()

        to_sibling(z).start()

    half_places = n_dp // 2

    def disp_to(i):
        to, at = receiver(i), i // 2 * 2 + core
        return dp_copy(disp_send.at[to], disp_recv.at[at], disp_ssem, disp_rsem.at[i // half_places], to)

    def several(buffer, count, send_sem, recv_sem):
        blocks_of = buffer.at[pl.ds(0, count)]
        return dp_copy(blocks_of, blocks_of, send_sem, recv_sem, sibling)

    start_ring()

    def part_to(j):
        return f_copy(part_send.at[j], part_recv.at[fs], part_ssem, part_rsem, j)

    def term(j):
        from_sibling(j).wait_recv()
        part_send[pl.ds(j, 1)] = jnp.concatenate(
            [jnp.dot(x_ref[...], wt_all[j, c, pl.ds(0, depth)], preferred_element_type=f32) for c in range(2)],
            axis=1,
        ).astype(bf16)[None]

        @pl.when(j == fs)
        def _():
            part_recv[pl.ds(j, 1)] = part_send[pl.ds(j, 1)]

        @pl.when(j != fs)
        def _():
            part_to(j).start()

    def from_left(step):
        return lax.rem(z + n_z - step, n_z)

    def from_right(step):
        return lax.rem(z + step, n_z)

    term(z)

    @pl.loop(1, half_z)
    def _(s):
        @pl.loop(0, PIECES)
        def _(q):
            ring_right(from_left(s), s, q).wait_recv()
            ring_right(from_left(s), s + 1, q).start()
            ring_left(from_right(s), s, q).wait_recv()

            @pl.when(s < half_z - 1)
            def _():
                ring_left(from_right(s), s + 1, q).start()

            @pl.when((s > 1) & (q != 1))
            def _():
                term(lax.rem(z + n_z + (s - 1) * (q - 1), n_z))

        to_sibling(from_left(s)).start()
        to_sibling(from_right(s)).start()

    places(0, n_dp, lambda i: disp_to(i).start())

    @pl.loop(0, PIECES)
    def _(q):
        ring_right(from_left(half_z), half_z, q).wait_recv()

    to_sibling(from_left(half_z)).start()

    @pl.loop(0, 3)
    def _(k):
        term(lax.rem(z + n_z + jnp.where(k == 0, 1 - half_z, half_z - 2 + k), n_z))

    first = iota((GROUP * chunk, 128), 1) < 64

    def tags_of(sources, lanes):
        each = []
        for source, lane in zip(sources, lanes):
            row = wt_all[source // 2, source % 2, pl.ds(depth, 16)].astype(f32)[:1]
            mine = iota((chunk, 128), 1) == lane + iota((chunk, 128), 0) // BLK
            tag = jnp.sum(jnp.where(mine, row, 0.0), axis=1, keepdims=True)
            each.append(jnp.broadcast_to(tag, (chunk, 128)))
        return jnp.concatenate(each, axis=0) > 0.5

    def got_tags(i):
        return tags_of([sender(i * GROUP + k) for k in range(GROUP)], [me * cap] * GROUP)

    def fold(value):
        value = value.reshape(GROUP, 2 * chunk, value.shape[1])
        return value[:, :chunk], value[:, chunk:]

    def projected(got, maps, half):
        one = lax.dot_general(got, maps[:, :half], contract_last, preferred_element_type=f32)
        two = lax.dot_general(got, maps[:, half:], contract_last, preferred_element_type=f32)
        return (fold(one)[0] + fold(two)[1]).reshape(GROUP * chunk, 128)

    def project(i):
        got = disp_recv[pl.ds(i * GROUP, GROUP)].reshape(GROUP * 2 * chunk, hs + hw)
        low = projected(got[:, :hs], d_ref[...], hs)
        back = projected(got[:, hs:], u_ref[...], hw)
        tag = got_tags(i)
        low = jnp.where(tag, pltpu.roll(low, 64, 1), low)
        back = jnp.where(tag, back, pltpu.roll(back, 64, 1))
        lr_send[pl.ds(i * 2, 2)] = jnp.where(first, low, back).reshape(2, 2 * chunk, 128).astype(bf16)

    def rs_to(j):
        return f_copy(lr_send.at[j], lr_recv.at[fs], rs_ssem, rs_rsem, j)

    def ag_to(j):
        return f_copy(lr_all.at[fs], lr_all.at[fs], ag_ssem, ag_rsem.at[fs // (n_f // 2)], j)

    def others(n, mine, act):
        @pl.loop(1, n)
        def _(k):
            act(lax.rem(mine + k, n))

    def but_me(start, stop, act):
        @pl.loop(start, stop)
        def _(j):
            @pl.when(j != fs)
            def _():
                act(j)

    def by_slot(value, tag):
        turned = pltpu.roll(value, 64, 1)
        low = jnp.where(first, jnp.where(tag, 0.0, value), jnp.where(tag, turned, 0.0))
        back = jnp.where(first, jnp.where(tag, 0.0, turned), jnp.where(tag, value, 0.0))
        return low, back

    def ranked(i):
        return lr_all[pl.ds(i * 2, 2)].reshape(GROUP * chunk, 128).astype(f32)

    def ret_to(i):
        to, at = sender(i), i // 2 * 2 + core
        return dp_copy(ret_send.at[i], ret_recv.at[at], ret_ssem, ret_rsem.at[i // half_places], to)

    def adapt(i):
        low, _ = by_slot(ranked(i), got_tags(i))
        adapted = adapter_scale * jnp.dot(low.astype(bf16), u_ref[...], preferred_element_type=f32)
        adapted = adapted.reshape(GROUP, chunk, width)
        ret_send[pl.ds(i * GROUP, GROUP)] = jnp.concatenate(
            [adapted[:, :, :hw], adapted[:, :, hw:]], axis=1
        ).astype(bf16)

    def take(i):
        one, two = fold(ret_recv[pl.ds(i * GROUP, GROUP)].astype(f32).reshape(GROUP * 2 * chunk, hw))
        value = jnp.concatenate([one, two], axis=2).reshape(GROUP * chunk, width).astype(bf16)
        goal = iota((1, GROUP * chunk), 1) % chunk
        place = iota((1, GROUP * chunk), 1) // chunk
        for k in range(GROUP):
            goal = jnp.where(place == k, goal + receiver(i * GROUP + k) * chunk, goal)
        pick = jnp.where(goal == row_target_col, 1.0, 0.0).astype(bf16)
        acc[...] += jnp.dot(pick, value, preferred_element_type=f32)

    def count(half):
        return half_places - half

    def arrive(half):
        several(disp_recv, count(half), disp_ssem, disp_rsem.at[half]).wait_recv()

    groups = n_dp // GROUP // 2

    def scatter(half):
        low_j, high_j = half * (n_f // 2), (half + 1) * (n_f // 2)
        pl.loop(half * groups, (half + 1) * groups)(project)
        but_me(low_j, high_j, lambda j: rs_to(j).start())

    def reduce(half):
        @pl.when(fs // (n_f // 2) == half)
        def _():
            lr_recv[pl.ds(fs, 1)] = lr_send[pl.ds(fs, 1)]
            several(lr_recv, n_f - 1, rs_ssem, rs_rsem).wait_recv()
            lr_all[pl.ds(fs, 1)] = jnp.sum(lr_recv[...].astype(f32), axis=0).astype(bf16)[None]
            others(n_f, fs, lambda j: ag_to(j).start())

    def give_back(half):
        mine = fs // (n_f // 2) == half
        for is_mine, chunks in ((True, n_f // 2 - 1), (False, n_f // 2)):
            @pl.when(mine == is_mine)
            def _():
                several(lr_all, chunks, ag_ssem, ag_rsem.at[half]).wait_recv()

        pl.loop(half * groups, (half + 1) * groups)(adapt)
        places(half * half_places, (half + 1) * half_places, lambda i: ret_to(i).start())

    def gradients(i):
        got = disp_recv[pl.ds(i * GROUP, GROUP)].reshape(GROUP * 2 * chunk, hs + hw)
        low, back = by_slot(ranked(i), got_tags(i))
        low = low.reshape(GROUP, chunk, 128)
        back = back.reshape(GROUP, chunk, 128)
        zero = jnp.zeros_like(low)

        def part(value, h, rows_of):
            pair = [value, zero] if h == 0 else [zero, value]
            wide = jnp.concatenate(pair, axis=1).reshape(GROUP * 2 * chunk, 128).astype(bf16)
            return lax.dot_general(wide, rows_of, contract_first, preferred_element_type=f32)

        for h in range(2):
            gd_ref[:, h * hs:(h + 1) * hs] += part(back, h, got[:, :hs])
            gu_ref[:, h * hw:(h + 1) * hw] += part(low, h, got[:, hs:])

    def ret_arrive(half):
        several(ret_recv, count(half), ret_ssem, ret_rsem.at[half]).wait_recv()
        pl.loop(half * groups, (half + 1) * groups)(take)

    arrive(0)
    scatter(0)
    reduce(0)
    give_back(0)
    gd_ref[...] = jnp.zeros_like(gd_ref)
    gu_ref[...] = jnp.zeros_like(gu_ref)
    arrive(1)
    scatter(1)

    several(part_recv, n_f - 1, part_ssem, part_rsem).wait_recv()
    acc[...] = part_recv[0].astype(f32)

    @pl.loop(1, n_f)
    def _(j):
        acc[...] += part_recv[j].astype(f32)

    reduce(1)
    pl.loop(0, groups)(gradients)
    give_back(1)
    ret_recv[pl.ds(last, 1)] = ret_send[pl.ds(last, 1)]
    pl.loop(groups, 2 * groups)(gradients)
    ret_arrive(0)
    ret_arrive(1)
    out_ref[...] = acc[...].astype(bf16)

    dp_copy(
        wt_all.at[pl.ds(0, half_z), 0], wt_all.at[pl.ds(0, half_z), 0], ring_r_send, ring_r_recv.at[0], right
    ).wait_send()
    dp_copy(
        wt_all.at[pl.ds(0, half_z - 1), 0], wt_all.at[pl.ds(0, half_z - 1), 0], ring_l_send, ring_l_recv.at[0], left
    ).wait_send()
    dp_copy(wt_all.at[:, 0], wt_all.at[:, 0], sib_send, sib_recv.at[0], sibling).wait_send()
    several(disp_send, n_dp - 1, disp_ssem, disp_rsem.at[0]).wait_send()
    several(part_send, n_f - 1, part_ssem, part_rsem).wait_send()
    several(lr_send, n_f - 1, rs_ssem, rs_rsem).wait_send()
    several(lr_all, n_f - 1, ag_ssem, ag_rsem.at[0]).wait_send()
    several(ret_send, n_dp - 1, ret_ssem, ret_rsem.at[0]).wait_send()


def fused(x, g, w, down, up, block_member, member_slot):
    n_dp, n_f = lax.axis_size("dp"), lax.axis_size("fsdp")
    rows, slab = x.shape
    width = g.shape[1]
    cap = 2 * block_member.shape[1] // n_dp
    chunk = cap * BLK
    n_z = n_dp // 2
    vmem = pl.BlockSpec(memory_space=pltpu.VMEM)
    hbm = pl.BlockSpec(memory_space=pltpu.HBM)
    dma = pltpu.SemaphoreType.DMA
    hops = (n_z // 2 + 1) * PIECES
    return pl.pallas_call(
        functools.partial(kernel, (n_dp, n_f, cap)),
        out_shape=(
            jax.ShapeDtypeStruct((rows, width), bf16),
            jax.ShapeDtypeStruct(down.shape, f32),
            jax.ShapeDtypeStruct(up.shape, f32),
        ),
        in_specs=[hbm] * 5 + [vmem] * 2,
        out_specs=(vmem,) * 3,
        scratch_shapes=[
            pltpu.VMEM(x.shape, bf16), pltpu.VMEM(g.shape, bf16),
            pltpu.VMEM(down.shape, bf16), pltpu.VMEM(up.shape, bf16),
            pltpu.VMEM((n_z, 2, w.shape[0] + 16, 128), bf16),
            pltpu.VMEM((n_dp, 2 * chunk, (slab + width) // 2), bf16),
            pltpu.VMEM((n_dp, 2 * chunk, (slab + width) // 2), bf16),
            pltpu.VMEM((n_f, rows, width), bf16),
            pltpu.VMEM((n_f, rows, width), bf16),
            pltpu.VMEM((n_f, 2 * chunk, 128), bf16),
            pltpu.VMEM((n_f, 2 * chunk, 128), bf16),
            pltpu.VMEM((n_f, 2 * chunk, 128), bf16),
            pltpu.VMEM((n_dp, 2 * chunk, width // 2), bf16),
            pltpu.VMEM((n_dp, 2 * chunk, width // 2), bf16),
            pltpu.VMEM((rows, width), f32),
            dma((5,)), dma, dma((hops,)), dma, dma((hops,)), dma, dma((n_z,)),
            dma, dma((2,)), dma, dma, dma, dma, dma, dma((2,)), dma, dma((2,)),
        ],
        compiler_params=pltpu.CompilerParams(
            collective_id=0, has_side_effects=True, vmem_limit_bytes=40 * 1024 * 1024
        ),
        name="adapter_step",
    )(x, g, w, down, up, block_member, member_slot)


def body(
    inputs, out_grad, base_weight, down_maps, up_maps,
    mean_down, square_down, mean_up, square_up, block_member, member_slot,
):
    owned, rank, slab_width = down_maps.shape
    out_width = up_maps.shape[2]
    projected, down_gradient, up_gradient = fused(
        inputs,
        out_grad,
        base_weight,
        down_maps.reshape(owned * rank, slab_width),
        up_maps.reshape(owned * rank, out_width),
        block_member.reshape(1, -1),
        member_slot.reshape(1, -1),
    )
    theta_down = down_maps.astype(f32) - (rate_down * adapter_scale) * down_gradient.reshape(down_maps.shape)
    theta_up = up_maps.astype(f32) - (rate_up * adapter_scale) * up_gradient.reshape(up_maps.shape)
    denominator = SNAPS + 1.0
    new_mean_down = (SNAPS * mean_down + theta_down) / denominator
    new_square_down = (SNAPS * square_down + theta_down * theta_down) / denominator
    new_mean_up = (SNAPS * mean_up + theta_up) / denominator
    new_square_up = (SNAPS * square_up + theta_up * theta_up) / denominator
    return (projected, new_mean_down, new_square_down, new_mean_up, new_square_up)


def solution(mesh):
    split = P("dp", None, "fsdp")
    placed = (P("dp", "fsdp"), P("dp", "fsdp"), P("fsdp", "dp")) + (split,) * 6 + (P("dp"), P())
    return jax.shard_map(
        body,
        mesh=mesh,
        in_specs=placed,
        out_specs=(P("dp", "fsdp"),) + (split,) * 4,
        check_vma=False,
    )
```

```python
import functools

import jax
import jax.numpy as jnp
from jax import lax
from jax.experimental import pallas as pl
from jax.experimental.pallas import tpu as pltpu
from jax.sharding import PartitionSpec as P

SNAPS = 2
BLK = 8

adapter_scale = 2.0
rate_down = 0.002
rate_up = 0.02
contract_last = (((1,), (1,)), ((), ()))
contract_first = (((0,), (0,)), ((), ()))
MESH = pl.DeviceIdType.MESH
GROUP = 4
PIECES = 3

f32 = jnp.float32
bf16 = jnp.bfloat16


def iota(shape, dim):
    return lax.broadcasted_iota(jnp.int32, shape, dim)


def to_column(row):
    n = row.shape[1]
    return jnp.sum(jnp.where(iota((n, n), 0) == iota((n, n), 1), row, 0), axis=1, keepdims=True)


def kernel(
    sizes,
    x_hbm, g_hbm, w_hbm, d_hbm, u_hbm, member_hbm, slot_hbm, md_hbm, sd_hbm, mu_hbm, su_hbm,
    out_ref, md_out, sd_out, mu_out, su_out,
    x_ref, g_ref, d_ref, u_ref, member_ref, slot_ref, md_ref, sd_ref, mu_ref, su_ref, gd_ref, gu_ref, wt_all, disp_send, disp_recv,
    part_send, part_recv, lr_send, lr_recv, lr_all, ret_send, ret_recv, acc,
    in_sem, ring_r_send, ring_r_recv, ring_l_send, ring_l_recv, sib_send, sib_recv,
    disp_ssem, disp_rsem, part_ssem, part_rsem,
    rs_ssem, rs_rsem, ag_ssem, ag_rsem, ret_ssem, ret_rsem,
):
    n_dp, n_f, cap = sizes
    n_z = n_dp // 2
    half_z = n_z // 2
    rows, slab = x_hbm.shape
    width = g_hbm.shape[1]
    hs, hw = slab // 2, width // 2
    blocks = member_hbm.shape[1]
    members = slot_hbm.shape[1]
    chunk = cap * BLK
    depth = w_hbm.shape[0]
    me = lax.axis_index("dp")
    fs = lax.axis_index("fsdp")
    z, core = me // 2, me % 2
    right = lax.rem(z + 1, n_z) * 2 + core
    left = lax.rem(z + n_z - 1, n_z) * 2 + core
    sibling = z * 2 + (1 - core)
    last = n_dp - 2 + core

    def offset(m):
        return jnp.where(m % 2 == 1, half_z - (m + 1) // 2, m // 2 + n_z - half_z)

    def receiver(i):
        return lax.rem(z + offset(i // 2), n_z) * 2 + i % 2

    def sender(i):
        return lax.rem(z + n_z - lax.rem(offset(i // 2), n_z), n_z) * 2 + i % 2

    def places(start, stop, act):
        @pl.loop(start, stop)
        def _(i):
            @pl.when(i != last)
            def _():
                act(i)

    def dp_copy(src, dst, send_sem, recv_sem, to):
        return pltpu.make_async_remote_copy(
            src_ref=src, dst_ref=dst, send_sem=send_sem, recv_sem=recv_sem,
            device_id=(to, fs), device_id_type=MESH,
        )

    def f_copy(src, dst, send_sem, recv_sem, to):
        return pltpu.make_async_remote_copy(
            src_ref=src, dst_ref=dst, send_sem=send_sem, recv_sem=recv_sem,
            device_id=(me, to), device_id_type=MESH,
        )

    barrier = pltpu.get_barrier_semaphore()
    loads = [
        pltpu.make_async_copy(src, dst, in_sem.at[i])
        for i, (src, dst) in enumerate(
            [
                (member_hbm, member_ref), (slot_hbm, slot_ref), (x_hbm, x_ref), (g_hbm, g_ref),
                (w_hbm, wt_all.at[z, core, pl.ds(0, depth)]), (d_hbm, d_ref), (u_hbm, u_ref),
                (md_hbm, md_ref), (sd_hbm, sd_ref), (mu_hbm, mu_ref), (su_hbm, su_ref),
            ]
        )
    ]
    for load in loads:
        load.start()

    @pl.loop(1, n_dp)
    def _(k):
        pl.semaphore_signal(barrier, inc=1, device_id=(lax.rem(me + k, n_dp), fs), device_id_type=MESH)

    @pl.loop(1, n_f)
    def _(k):
        pl.semaphore_signal(barrier, inc=1, device_id=(me, lax.rem(fs + k, n_f)), device_id_type=MESH)

    for load in loads[:2]:
        load.wait()

    slot_col = to_column(slot_ref[...])
    slots = jnp.sum(
        jnp.where(iota((members, blocks), 0) == member_ref[...], slot_col, 0), axis=0, keepdims=True
    )
    owner = slots // 2
    local = slots - owner * 2
    owner_col = to_column(owner)
    earlier = (owner_col == owner) & (iota((blocks, blocks), 0) < iota((blocks, blocks), 1))
    position = jnp.sum(jnp.where(earlier, 1, 0), axis=0, keepdims=True)
    target = owner * cap + position
    target_col = to_column(target)
    local_col = to_column(local)
    row_target = (
        jnp.sum(
            jnp.where(iota((blocks, rows), 0) == iota((blocks, rows), 1) // BLK, target_col, 0),
            axis=0, keepdims=True,
        ) * BLK
        + iota((1, rows), 1) % BLK
    )
    row_target_col = (
        jnp.sum(
            jnp.where(iota((rows, blocks), 1) == iota((rows, blocks), 0) // BLK, target, 0),
            axis=1, keepdims=True,
        ) * BLK
        + iota((rows, 1), 0) % BLK
    )
    tags = jnp.sum(
        jnp.where(target_col == iota((blocks, 128), 1), local_col, 0), axis=0, keepdims=True
    )
    wt_all[pl.ds(z, 1), pl.ds(core, 1), pl.ds(depth, 16)] = jnp.broadcast_to(
        tags.astype(f32), (16, 128)
    ).astype(bf16)[None, None]
    for load in loads[2:7]:
        load.wait()

    pl.semaphore_wait(barrier, n_dp + n_f - 2)

    piece = wt_all.shape[2] // PIECES

    def ring_right(src_z, step, q):
        block = wt_all.at[src_z, core, pl.ds(pl.multiple_of(q * piece, piece), piece)]
        at = step * PIECES + q
        return dp_copy(block, block, ring_r_send, ring_r_recv.at[at], right)

    def ring_left(src_z, step, q):
        block = wt_all.at[src_z, core, pl.ds(pl.multiple_of(q * piece, piece), piece)]
        at = step * PIECES + q
        return dp_copy(block, block, ring_l_send, ring_l_recv.at[at], left)

    def to_sibling(src_z):
        block = wt_all.at[src_z, core]
        return dp_copy(block, block, sib_send, sib_recv.at[src_z], sibling)

    def from_sibling(src_z):
        block = wt_all.at[src_z, 1 - core]
        return dp_copy(block, block, sib_send, sib_recv.at[src_z], sibling)

    def start_ring():
        @pl.loop(0, PIECES)
        def _(q):
            ring_right(z, 1, q).start()
            ring_left(z, 1, q).start()

        to_sibling(z).start()

    half_places = n_dp // 2

    def disp_to(i):
        to, at = receiver(i), i // 2 * 2 + core
        return dp_copy(disp_send.at[to], disp_recv.at[at], disp_ssem, disp_rsem.at[i // half_places], to)

    def several(buffer, count, send_sem, recv_sem):
        blocks_of = buffer.at[pl.ds(0, count)]
        return dp_copy(blocks_of, blocks_of, send_sem, recv_sem, sibling)

    start_ring()

    halves = [
        jnp.concatenate([x_ref[:, h * hs:(h + 1) * hs], g_ref[:, h * hw:(h + 1) * hw]], axis=1)
        for h in range(2)
    ]

    @pl.loop(0, n_dp // GROUP)
    def _(i):
        pick = jnp.where(
            iota((GROUP * chunk, rows), 0) + i * (GROUP * chunk) == row_target, 1.0, 0.0
        ).astype(bf16)
        both = [
            jnp.dot(pick, half, preferred_element_type=f32).reshape(GROUP, chunk, hs + hw)
            for half in halves
        ]
        disp_send[pl.ds(i * GROUP, GROUP)] = jnp.concatenate(both, axis=1).astype(bf16)

    disp_recv[pl.ds(last, 1)] = disp_send[pl.ds(me, 1)]

    def part_to(j):
        return f_copy(part_send.at[j], part_recv.at[fs], part_ssem, part_rsem, j)

    def term(j):
        from_sibling(j).wait_recv()
        part_send[pl.ds(j, 1)] = jnp.concatenate(
            [jnp.dot(x_ref[...], wt_all[j, c, pl.ds(0, depth)], preferred_element_type=f32) for c in range(2)],
            axis=1,
        ).astype(bf16)[None]

        @pl.when(j == fs)
        def _():
            part_recv[pl.ds(j, 1)] = part_send[pl.ds(j, 1)]

        @pl.when(j != fs)
        def _():
            part_to(j).start()

    def from_left(step):
        return lax.rem(z + n_z - step, n_z)

    def from_right(step):
        return lax.rem(z + step, n_z)

    term(z)

    @pl.loop(1, half_z)
    def _(s):
        @pl.loop(0, PIECES)
        def _(q):
            ring_right(from_left(s), s, q).wait_recv()
            ring_right(from_left(s), s + 1, q).start()
            ring_left(from_right(s), s, q).wait_recv()

            @pl.when(s < half_z - 1)
            def _():
                ring_left(from_right(s), s + 1, q).start()

            @pl.when((s > 1) & (q != 1))
            def _():
                term(lax.rem(z + n_z + (s - 1) * (q - 1), n_z))

        to_sibling(from_left(s)).start()
        to_sibling(from_right(s)).start()

    places(0, n_dp, lambda i: disp_to(i).start())

    @pl.loop(0, PIECES)
    def _(q):
        ring_right(from_left(half_z), half_z, q).wait_recv()

    to_sibling(from_left(half_z)).start()

    @pl.loop(0, 3)
    def _(k):
        term(lax.rem(z + n_z + jnp.where(k == 0, 1 - half_z, half_z - 2 + k), n_z))

    first = iota((GROUP * chunk, 128), 1) < 64

    def tags_of(sources, lanes):
        each = []
        for source, lane in zip(sources, lanes):
            row = wt_all[source // 2, source % 2, pl.ds(depth, 16)].astype(f32)[:1]
            mine = iota((chunk, 128), 1) == lane + iota((chunk, 128), 0) // BLK
            tag = jnp.sum(jnp.where(mine, row, 0.0), axis=1, keepdims=True)
            each.append(jnp.broadcast_to(tag, (chunk, 128)))
        return jnp.concatenate(each, axis=0) > 0.5

    def got_tags(i):
        return tags_of([sender(i * GROUP + k) for k in range(GROUP)], [me * cap] * GROUP)

    def fold(value):
        value = value.reshape(GROUP, 2 * chunk, value.shape[1])
        return value[:, :chunk], value[:, chunk:]

    def projected(got, maps, half):
        one = lax.dot_general(got, maps[:, :half], contract_last, preferred_element_type=f32)
        two = lax.dot_general(got, maps[:, half:], contract_last, preferred_element_type=f32)
        return (fold(one)[0] + fold(two)[1]).reshape(GROUP * chunk, 128)

    def project(i):
        got = disp_recv[pl.ds(i * GROUP, GROUP)].reshape(GROUP * 2 * chunk, hs + hw)
        low = projected(got[:, :hs], d_ref[...], hs)
        back = projected(got[:, hs:], u_ref[...], hw)
        tag = got_tags(i)
        low = jnp.where(tag, pltpu.roll(low, 64, 1), low)
        back = jnp.where(tag, back, pltpu.roll(back, 64, 1))
        lr_send[pl.ds(i * 2, 2)] = jnp.where(first, low, back).reshape(2, 2 * chunk, 128).astype(bf16)

    def rs_to(j):
        return f_copy(lr_send.at[j], lr_recv.at[fs], rs_ssem, rs_rsem, j)

    def ag_to(j):
        return f_copy(lr_all.at[fs], lr_all.at[fs], ag_ssem, ag_rsem.at[fs // (n_f // 2)], j)

    def others(n, mine, act):
        @pl.loop(1, n)
        def _(k):
            act(lax.rem(mine + k, n))

    def but_me(start, stop, act):
        @pl.loop(start, stop)
        def _(j):
            @pl.when(j != fs)
            def _():
                act(j)

    def by_slot(value, tag):
        turned = pltpu.roll(value, 64, 1)
        low = jnp.where(first, jnp.where(tag, 0.0, value), jnp.where(tag, turned, 0.0))
        back = jnp.where(first, jnp.where(tag, 0.0, turned), jnp.where(tag, value, 0.0))
        return low, back

    def ranked(i):
        return lr_all[pl.ds(i * 2, 2)].reshape(GROUP * chunk, 128).astype(f32)

    def ret_to(i):
        to, at = sender(i), i // 2 * 2 + core
        return dp_copy(ret_send.at[i], ret_recv.at[at], ret_ssem, ret_rsem.at[i // half_places], to)

    def adapt(i):
        low, _ = by_slot(ranked(i), got_tags(i))
        adapted = adapter_scale * jnp.dot(low.astype(bf16), u_ref[...], preferred_element_type=f32)
        adapted = adapted.reshape(GROUP, chunk, width)
        ret_send[pl.ds(i * GROUP, GROUP)] = jnp.concatenate(
            [adapted[:, :, :hw], adapted[:, :, hw:]], axis=1
        ).astype(bf16)

    def take(i):
        one, two = fold(ret_recv[pl.ds(i * GROUP, GROUP)].astype(f32).reshape(GROUP * 2 * chunk, hw))
        value = jnp.concatenate([one, two], axis=2).reshape(GROUP * chunk, width).astype(bf16)
        goal = iota((1, GROUP * chunk), 1) % chunk
        place = iota((1, GROUP * chunk), 1) // chunk
        for k in range(GROUP):
            goal = jnp.where(place == k, goal + receiver(i * GROUP + k) * chunk, goal)
        pick = jnp.where(goal == row_target_col, 1.0, 0.0).astype(bf16)
        acc[...] += jnp.dot(pick, value, preferred_element_type=f32)

    def count(half):
        return half_places - half

    def arrive(half):
        several(disp_recv, count(half), disp_ssem, disp_rsem.at[half]).wait_recv()

    groups = n_dp // GROUP // 2

    def scatter(half):
        low_j, high_j = half * (n_f // 2), (half + 1) * (n_f // 2)
        pl.loop(half * groups, (half + 1) * groups)(project)
        but_me(low_j, high_j, lambda j: rs_to(j).start())

    def reduce(half):
        @pl.when(fs // (n_f // 2) == half)
        def _():
            lr_recv[pl.ds(fs, 1)] = lr_send[pl.ds(fs, 1)]
            several(lr_recv, n_f - 1, rs_ssem, rs_rsem).wait_recv()
            lr_all[pl.ds(fs, 1)] = jnp.sum(lr_recv[...].astype(f32), axis=0).astype(bf16)[None]
            others(n_f, fs, lambda j: ag_to(j).start())

    def give_back(half):
        mine = fs // (n_f // 2) == half
        for is_mine, chunks in ((True, n_f // 2 - 1), (False, n_f // 2)):
            @pl.when(mine == is_mine)
            def _():
                several(lr_all, chunks, ag_ssem, ag_rsem.at[half]).wait_recv()

        pl.loop(half * groups, (half + 1) * groups)(adapt)
        places(half * half_places, (half + 1) * half_places, lambda i: ret_to(i).start())

    def gradients(i):
        got = disp_recv[pl.ds(i * GROUP, GROUP)].reshape(GROUP * 2 * chunk, hs + hw)
        low, back = by_slot(ranked(i), got_tags(i))
        low = low.reshape(GROUP, chunk, 128)
        back = back.reshape(GROUP, chunk, 128)
        zero = jnp.zeros_like(low)

        def part(value, h, rows_of):
            pair = [value, zero] if h == 0 else [zero, value]
            wide = jnp.concatenate(pair, axis=1).reshape(GROUP * 2 * chunk, 128).astype(bf16)
            return lax.dot_general(wide, rows_of, contract_first, preferred_element_type=f32)

        for h in range(2):
            gd_ref[:, h * hs:(h + 1) * hs] += part(back, h, got[:, :hs])
            gu_ref[:, h * hw:(h + 1) * hw] += part(low, h, got[:, hs:])

    def ret_arrive(half):
        several(ret_recv, count(half), ret_ssem, ret_rsem.at[half]).wait_recv()
        pl.loop(half * groups, (half + 1) * groups)(take)

    arrive(0)
    scatter(0)
    reduce(0)
    give_back(0)
    gd_ref[...] = jnp.zeros_like(gd_ref)
    gu_ref[...] = jnp.zeros_like(gu_ref)
    arrive(1)
    scatter(1)

    several(part_recv, n_f - 1, part_ssem, part_rsem).wait_recv()
    acc[...] = part_recv[0].astype(f32)

    @pl.loop(1, n_f)
    def _(j):
        acc[...] += part_recv[j].astype(f32)

    reduce(1)
    pl.loop(0, groups)(gradients)
    give_back(1)
    ret_recv[pl.ds(last, 1)] = ret_send[pl.ds(last, 1)]
    pl.loop(groups, 2 * groups)(gradients)

    for load in loads[7:]:
        load.wait()
    for maps, rate, grad, mean, square, new_mean, new_square in (
        (d_ref, rate_down, gd_ref, md_ref, sd_ref, md_out, sd_out),
        (u_ref, rate_up, gu_ref, mu_ref, su_ref, mu_out, su_out),
    ):
        theta = maps[...].astype(f32) - (rate * adapter_scale) * grad[...]
        new_mean[...] = (SNAPS * mean[...] + theta) / (SNAPS + 1.0)
        new_square[...] = (SNAPS * square[...] + theta * theta) / (SNAPS + 1.0)

    ret_arrive(0)
    ret_arrive(1)
    out_ref[...] = acc[...].astype(bf16)

    dp_copy(
        wt_all.at[pl.ds(0, half_z), 0], wt_all.at[pl.ds(0, half_z), 0], ring_r_send, ring_r_recv.at[0], right
    ).wait_send()
    dp_copy(
        wt_all.at[pl.ds(0, half_z - 1), 0], wt_all.at[pl.ds(0, half_z - 1), 0], ring_l_send, ring_l_recv.at[0], left
    ).wait_send()
    dp_copy(wt_all.at[:, 0], wt_all.at[:, 0], sib_send, sib_recv.at[0], sibling).wait_send()
    several(disp_send, n_dp - 1, disp_ssem, disp_rsem.at[0]).wait_send()
    several(part_send, n_f - 1, part_ssem, part_rsem).wait_send()
    several(lr_send, n_f - 1, rs_ssem, rs_rsem).wait_send()
    several(lr_all, n_f - 1, ag_ssem, ag_rsem.at[0]).wait_send()
    several(ret_send, n_dp - 1, ret_ssem, ret_rsem.at[0]).wait_send()


def fused(x, g, w, down, up, block_member, member_slot, *moments):
    n_dp, n_f = lax.axis_size("dp"), lax.axis_size("fsdp")
    rows, slab = x.shape
    width = g.shape[1]
    cap = 2 * block_member.shape[1] // n_dp
    chunk = cap * BLK
    n_z = n_dp // 2
    vmem = pl.BlockSpec(memory_space=pltpu.VMEM)
    hbm = pl.BlockSpec(memory_space=pltpu.HBM)
    dma = pltpu.SemaphoreType.DMA
    hops = (n_z // 2 + 1) * PIECES
    return pl.pallas_call(
        functools.partial(kernel, (n_dp, n_f, cap)),
        out_shape=(
            jax.ShapeDtypeStruct((rows, width), bf16),
        )
        + tuple(jax.ShapeDtypeStruct(moment.shape, f32) for moment in moments),
        in_specs=[hbm] * 11,
        out_specs=(vmem,) * 5,
        scratch_shapes=[
            pltpu.VMEM(x.shape, bf16), pltpu.VMEM(g.shape, bf16),
            pltpu.VMEM(down.shape, bf16), pltpu.VMEM(up.shape, bf16),
            pltpu.VMEM(block_member.shape, jnp.int32), pltpu.VMEM(member_slot.shape, jnp.int32),
            *(pltpu.VMEM(moment.shape, f32) for moment in moments),
            pltpu.VMEM(down.shape, f32), pltpu.VMEM(up.shape, f32),
            pltpu.VMEM((n_z, 2, w.shape[0] + 16, 128), bf16),
            pltpu.VMEM((n_dp, 2 * chunk, (slab + width) // 2), bf16),
            pltpu.VMEM((n_dp, 2 * chunk, (slab + width) // 2), bf16),
            pltpu.VMEM((n_f, rows, width), bf16),
            pltpu.VMEM((n_f, rows, width), bf16),
            pltpu.VMEM((n_f, 2 * chunk, 128), bf16),
            pltpu.VMEM((n_f, 2 * chunk, 128), bf16),
            pltpu.VMEM((n_f, 2 * chunk, 128), bf16),
            pltpu.VMEM((n_dp, 2 * chunk, width // 2), bf16),
            pltpu.VMEM((n_dp, 2 * chunk, width // 2), bf16),
            pltpu.VMEM((rows, width), f32),
            dma((11,)), dma, dma((hops,)), dma, dma((hops,)), dma, dma((n_z,)),
            dma, dma((2,)), dma, dma, dma, dma, dma, dma((2,)), dma, dma((2,)),
        ],
        compiler_params=pltpu.CompilerParams(
            collective_id=0, has_side_effects=True, vmem_limit_bytes=60 * 1024 * 1024
        ),
        name="adapter_step",
    )(x, g, w, down, up, block_member, member_slot, *moments)


def settle(*results):
    n = len(results)

    def move(*refs):
        here, sems = refs[2 * n:3 * n], refs[-1]
        loads = [pltpu.make_async_copy(refs[i], here[i], sems.at[i]) for i in range(n)]
        stores = [pltpu.make_async_copy(here[i], refs[n + i], sems.at[n + i]) for i in range(n)]
        for load in loads:
            load.start()
        for load, store in zip(loads, stores):
            load.wait()
            store.start()
        for store in stores:
            store.wait()

    anywhere = pl.BlockSpec(memory_space=pl.ANY)
    return pl.pallas_call(
        move,
        out_shape=tuple(jax.ShapeDtypeStruct(r.shape, r.dtype) for r in results),
        in_specs=[anywhere] * n,
        out_specs=(anywhere,) * n,
        scratch_shapes=[*(pltpu.VMEM(r.shape, r.dtype) for r in results), pltpu.SemaphoreType.DMA((2 * n,))],
        name="settle",
    )(*results)


def body(
    inputs, out_grad, base_weight, down_maps, up_maps,
    mean_down, square_down, mean_up, square_up, block_member, member_slot,
):
    maps = (down_maps, up_maps)
    moments = (mean_down, square_down, mean_up, square_up)

    def flat(value):
        return value.reshape(-1, value.shape[2])

    projected, *news = settle(
        *fused(
            inputs, out_grad, base_weight, *map(flat, maps),
            block_member.reshape(1, -1), member_slot.reshape(1, -1), *map(flat, moments),
        )
    )
    return (projected, *(new.reshape(old.shape) for new, old in zip(news, moments)))


def solution(mesh):
    split = P("dp", None, "fsdp")
    placed = (P("dp", "fsdp"), P("dp", "fsdp"), P("fsdp", "dp")) + (split,) * 6 + (P("dp"), P())
    return jax.shard_map(
        body,
        mesh=mesh,
        in_specs=placed,
        out_specs=(P("dp", "fsdp"),) + (split,) * 4,
        check_vma=False,
    )
```

```python
import functools

import jax
import jax.numpy as jnp
from jax import lax
from jax.experimental import pallas as pl
from jax.experimental.pallas import tpu as pltpu
from jax.sharding import PartitionSpec as P

SNAPS = 2
BLK = 8

adapter_scale = 2.0
rate_down = 0.002
rate_up = 0.02
contract_last = (((1,), (1,)), ((), ()))
contract_first = (((0,), (0,)), ((), ()))
MESH = pl.DeviceIdType.MESH
GROUP = 4
PIECES = 3

f32 = jnp.float32
bf16 = jnp.bfloat16


def iota(shape, dim):
    return lax.broadcasted_iota(jnp.int32, shape, dim)


def to_column(row):
    n = row.shape[1]
    return jnp.sum(jnp.where(iota((n, n), 0) == iota((n, n), 1), row, 0), axis=1, keepdims=True)


def kernel(
    sizes,
    x_hbm, g_hbm, w_hbm, d_hbm, u_hbm, member_hbm, slot_hbm, md_hbm, sd_hbm, mu_hbm, su_hbm,
    out_ref, md_out, sd_out, mu_out, su_out,
    x_ref, g_ref, d_ref, u_ref, member_ref, slot_ref, md_ref, sd_ref, mu_ref, su_ref, gd_ref, gu_ref, wt_all, disp_send, disp_recv,
    part_send, part_recv, lr_send, lr_recv, lr_all, ret_send, ret_recv, acc,
    in_sem, ring_r_send, ring_r_recv, ring_l_send, ring_l_recv, sib_send, sib_recv,
    disp_ssem, disp_rsem, part_ssem, part_rsem,
    rs_ssem, rs_rsem, ag_ssem, ag_rsem, ret_ssem, ret_rsem,
):
    n_dp, n_f, cap = sizes
    n_z = n_dp // 2
    half_z = n_z // 2
    rows, slab = x_hbm.shape
    width = g_hbm.shape[1]
    hs, hw = slab // 2, width // 2
    blocks = member_hbm.shape[1]
    members = slot_hbm.shape[1]
    chunk = cap * BLK
    depth = w_hbm.shape[0]
    me = lax.axis_index("dp")
    fs = lax.axis_index("fsdp")
    z, core = me // 2, me % 2
    right = lax.rem(z + 1, n_z) * 2 + core
    left = lax.rem(z + n_z - 1, n_z) * 2 + core
    sibling = z * 2 + (1 - core)
    last = n_dp - 2 + core

    def offset(m):
        return jnp.where(m % 2 == 1, half_z - (m + 1) // 2, m // 2 + n_z - half_z)

    def receiver(i):
        return lax.rem(z + offset(i // 2), n_z) * 2 + i % 2

    def sender(i):
        return lax.rem(z + n_z - lax.rem(offset(i // 2), n_z), n_z) * 2 + i % 2

    def places(start, stop, act):
        @pl.loop(start, stop)
        def _(i):
            @pl.when(i != last)
            def _():
                act(i)

    def dp_copy(src, dst, send_sem, recv_sem, to):
        return pltpu.make_async_remote_copy(
            src_ref=src, dst_ref=dst, send_sem=send_sem, recv_sem=recv_sem,
            device_id=(to, fs), device_id_type=MESH,
        )

    def f_copy(src, dst, send_sem, recv_sem, to):
        return pltpu.make_async_remote_copy(
            src_ref=src, dst_ref=dst, send_sem=send_sem, recv_sem=recv_sem,
            device_id=(me, to), device_id_type=MESH,
        )

    barrier = pltpu.get_barrier_semaphore()
    loads = [
        pltpu.make_async_copy(src, dst, in_sem.at[i])
        for i, (src, dst) in enumerate(
            [
                (member_hbm, member_ref), (slot_hbm, slot_ref), (x_hbm, x_ref), (g_hbm, g_ref),
                (w_hbm, wt_all.at[z, core, pl.ds(0, depth)]), (d_hbm, d_ref), (u_hbm, u_ref),
                (md_hbm, md_ref), (sd_hbm, sd_ref), (mu_hbm, mu_ref), (su_hbm, su_ref),
            ]
        )
    ]
    for load in loads:
        load.start()

    @pl.loop(1, n_dp)
    def _(k):
        pl.semaphore_signal(barrier, inc=1, device_id=(lax.rem(me + k, n_dp), fs), device_id_type=MESH)

    @pl.loop(1, n_f)
    def _(k):
        pl.semaphore_signal(barrier, inc=1, device_id=(me, lax.rem(fs + k, n_f)), device_id_type=MESH)

    for load in loads[:2]:
        load.wait()

    slot_col = to_column(slot_ref[...])
    slots = jnp.sum(
        jnp.where(iota((members, blocks), 0) == member_ref[...], slot_col, 0), axis=0, keepdims=True
    )
    owner = slots // 2
    local = slots - owner * 2
    owner_col = to_column(owner)
    earlier = (owner_col == owner) & (iota((blocks, blocks), 0) < iota((blocks, blocks), 1))
    position = jnp.sum(jnp.where(earlier, 1, 0), axis=0, keepdims=True)
    target = owner * cap + position
    target_col = to_column(target)
    local_col = to_column(local)
    row_target = (
        jnp.sum(
            jnp.where(iota((blocks, rows), 0) == iota((blocks, rows), 1) // BLK, target_col, 0),
            axis=0, keepdims=True,
        ) * BLK
        + iota((1, rows), 1) % BLK
    )
    row_target_col = (
        jnp.sum(
            jnp.where(iota((rows, blocks), 1) == iota((rows, blocks), 0) // BLK, target, 0),
            axis=1, keepdims=True,
        ) * BLK
        + iota((rows, 1), 0) % BLK
    )
    tags = jnp.sum(
        jnp.where(target_col == iota((blocks, 128), 1), local_col, 0), axis=0, keepdims=True
    )
    wt_all[pl.ds(z, 1), pl.ds(core, 1), pl.ds(depth, 16)] = jnp.broadcast_to(
        tags.astype(f32), (16, 128)
    ).astype(bf16)[None, None]
    for load in loads[2:7]:
        load.wait()

    pl.semaphore_wait(barrier, n_dp + n_f - 2)

    piece = wt_all.shape[2] // PIECES

    def ring_right(src_z, step, q):
        block = wt_all.at[src_z, core, pl.ds(pl.multiple_of(q * piece, piece), piece)]
        at = step * PIECES + q
        return dp_copy(block, block, ring_r_send, ring_r_recv.at[at], right)

    def ring_left(src_z, step, q):
        block = wt_all.at[src_z, core, pl.ds(pl.multiple_of(q * piece, piece), piece)]
        at = step * PIECES + q
        return dp_copy(block, block, ring_l_send, ring_l_recv.at[at], left)

    def to_sibling(src_z):
        block = wt_all.at[src_z, core]
        return dp_copy(block, block, sib_send, sib_recv.at[src_z], sibling)

    def from_sibling(src_z):
        block = wt_all.at[src_z, 1 - core]
        return dp_copy(block, block, sib_send, sib_recv.at[src_z], sibling)

    def start_ring():
        @pl.loop(0, PIECES)
        def _(q):
            ring_right(z, 1, q).start()
            ring_left(z, 1, q).start()

        to_sibling(z).start()

    half_places = n_dp // 2

    def disp_to(i):
        to, at = receiver(i), i // 2 * 2 + core
        return dp_copy(disp_send.at[to], disp_recv.at[at], disp_ssem, disp_rsem.at[i // GROUP], to)

    def several(buffer, count, send_sem, recv_sem):
        blocks_of = buffer.at[pl.ds(0, count)]
        return dp_copy(blocks_of, blocks_of, send_sem, recv_sem, sibling)

    start_ring()

    halves = [
        jnp.concatenate([x_ref[:, h * hs:(h + 1) * hs], g_ref[:, h * hw:(h + 1) * hw]], axis=1)
        for h in range(2)
    ]

    @pl.loop(0, n_dp // GROUP)
    def _(i):
        pick = jnp.where(
            iota((GROUP * chunk, rows), 0) + i * (GROUP * chunk) == row_target, 1.0, 0.0
        ).astype(bf16)
        both = [
            jnp.dot(pick, half, preferred_element_type=f32).reshape(GROUP, chunk, hs + hw)
            for half in halves
        ]
        disp_send[pl.ds(i * GROUP, GROUP)] = jnp.concatenate(both, axis=1).astype(bf16)

    disp_recv[pl.ds(last, 1)] = disp_send[pl.ds(me, 1)]

    def part_to(j):
        return f_copy(part_send.at[j], part_recv.at[fs], part_ssem, part_rsem, j)

    def term(j):
        from_sibling(j).wait_recv()
        part_send[pl.ds(j, 1)] = jnp.concatenate(
            [jnp.dot(x_ref[...], wt_all[j, c, pl.ds(0, depth)], preferred_element_type=f32) for c in range(2)],
            axis=1,
        ).astype(bf16)[None]

        @pl.when(j == fs)
        def _():
            part_recv[pl.ds(j, 1)] = part_send[pl.ds(j, 1)]

        @pl.when(j != fs)
        def _():
            part_to(j).start()

    def from_left(step):
        return lax.rem(z + n_z - step, n_z)

    def from_right(step):
        return lax.rem(z + step, n_z)

    term(z)

    @pl.loop(1, half_z)
    def _(s):
        @pl.loop(0, PIECES)
        def _(q):
            ring_right(from_left(s), s, q).wait_recv()
            ring_right(from_left(s), s + 1, q).start()
            ring_left(from_right(s), s, q).wait_recv()

            @pl.when(s < half_z - 1)
            def _():
                ring_left(from_right(s), s + 1, q).start()

            @pl.when((s > 1) & (q != 1))
            def _():
                term(lax.rem(z + n_z + (s - 1) * (q - 1), n_z))

        to_sibling(from_left(s)).start()
        to_sibling(from_right(s)).start()

    places(0, n_dp, lambda i: disp_to(i).start())

    @pl.loop(0, PIECES)
    def _(q):
        ring_right(from_left(half_z), half_z, q).wait_recv()

    to_sibling(from_left(half_z)).start()

    @pl.loop(0, 3)
    def _(k):
        term(lax.rem(z + n_z + jnp.where(k == 0, 1 - half_z, half_z - 2 + k), n_z))

    first = iota((GROUP * chunk, 128), 1) < 64

    def tags_of(sources, lanes):
        each = []
        for source, lane in zip(sources, lanes):
            row = wt_all[source // 2, source % 2, pl.ds(depth, 16)].astype(f32)[:1]
            mine = iota((chunk, 128), 1) == lane + iota((chunk, 128), 0) // BLK
            tag = jnp.sum(jnp.where(mine, row, 0.0), axis=1, keepdims=True)
            each.append(jnp.broadcast_to(tag, (chunk, 128)))
        return jnp.concatenate(each, axis=0) > 0.5

    def got_tags(i):
        return tags_of([sender(i * GROUP + k) for k in range(GROUP)], [me * cap] * GROUP)

    def fold(value):
        value = value.reshape(GROUP, 2 * chunk, value.shape[1])
        return value[:, :chunk], value[:, chunk:]

    def projected(got, maps, half):
        one = lax.dot_general(got, maps[:, :half], contract_last, preferred_element_type=f32)
        two = lax.dot_general(got, maps[:, half:], contract_last, preferred_element_type=f32)
        return (fold(one)[0] + fold(two)[1]).reshape(GROUP * chunk, 128)

    def project(i):
        got = disp_recv[pl.ds(i * GROUP, GROUP)].reshape(GROUP * 2 * chunk, hs + hw)
        low = projected(got[:, :hs], d_ref[...], hs)
        back = projected(got[:, hs:], u_ref[...], hw)
        tag = got_tags(i)
        low = jnp.where(tag, pltpu.roll(low, 64, 1), low)
        back = jnp.where(tag, back, pltpu.roll(back, 64, 1))
        lr_send[pl.ds(i * 2, 2)] = jnp.where(first, low, back).reshape(2, 2 * chunk, 128).astype(bf16)

    def rs_to(j):
        return f_copy(lr_send.at[j], lr_recv.at[fs], rs_ssem, rs_rsem, j)

    def ag_to(j):
        return f_copy(lr_all.at[fs], lr_all.at[fs], ag_ssem, ag_rsem.at[fs], j)

    def ag_from(j):
        return f_copy(lr_all.at[j], lr_all.at[j], ag_ssem, ag_rsem.at[j], j)

    def others(n, mine, act):
        @pl.loop(1, n)
        def _(k):
            act(lax.rem(mine + k, n))

    def but_me(start, stop, act):
        @pl.loop(start, stop)
        def _(j):
            @pl.when(j != fs)
            def _():
                act(j)

    def by_slot(value, tag):
        turned = pltpu.roll(value, 64, 1)
        low = jnp.where(first, jnp.where(tag, 0.0, value), jnp.where(tag, turned, 0.0))
        back = jnp.where(first, jnp.where(tag, 0.0, turned), jnp.where(tag, value, 0.0))
        return low, back

    def ranked(i):
        return lr_all[pl.ds(i * 2, 2)].reshape(GROUP * chunk, 128).astype(f32)

    def ret_to(i):
        to, at = sender(i), i // 2 * 2 + core
        return dp_copy(ret_send.at[i], ret_recv.at[at], ret_ssem, ret_rsem.at[i // GROUP], to)

    def adapt(i):
        low, _ = by_slot(ranked(i), got_tags(i))
        adapted = adapter_scale * jnp.dot(low.astype(bf16), u_ref[...], preferred_element_type=f32)
        adapted = adapted.reshape(GROUP, chunk, width)
        ret_send[pl.ds(i * GROUP, GROUP)] = jnp.concatenate(
            [adapted[:, :, :hw], adapted[:, :, hw:]], axis=1
        ).astype(bf16)

    def take(i):
        one, two = fold(ret_recv[pl.ds(i * GROUP, GROUP)].astype(f32).reshape(GROUP * 2 * chunk, hw))
        value = jnp.concatenate([one, two], axis=2).reshape(GROUP * chunk, width).astype(bf16)
        goal = iota((1, GROUP * chunk), 1) % chunk
        place = iota((1, GROUP * chunk), 1) // chunk
        for k in range(GROUP):
            goal = jnp.where(place == k, goal + receiver(i * GROUP + k) * chunk, goal)
        pick = jnp.where(goal == row_target_col, 1.0, 0.0).astype(bf16)
        acc[...] += jnp.dot(pick, value, preferred_element_type=f32)

    def arrived(i, buffer, send_sem, recv_sem):
        own = i == n_dp // GROUP - 1
        for is_own in (True, False):
            @pl.when(own == is_own)
            def _():
                several(buffer, GROUP - is_own, send_sem, recv_sem.at[i]).wait_recv()

    groups = n_dp // GROUP // 2

    def scatter(half):
        @pl.loop(half * groups, (half + 1) * groups)
        def _(i):
            arrived(i, disp_recv, disp_ssem, disp_rsem)
            project(i)
            but_me(2 * i, 2 * i + 2, lambda j: rs_to(j).start())

    def reduce(half):
        @pl.when(fs // (n_f // 2) == half)
        def _():
            lr_recv[pl.ds(fs, 1)] = lr_send[pl.ds(fs, 1)]
            several(lr_recv, n_f - 1, rs_ssem, rs_rsem).wait_recv()
            lr_all[pl.ds(fs, 1)] = jnp.sum(lr_recv[...].astype(f32), axis=0).astype(bf16)[None]
            others(n_f, fs, lambda j: ag_to(j).start())

    def give_back(half):
        @pl.loop(half * groups, (half + 1) * groups)
        def _(i):
            but_me(2 * i, 2 * i + 2, lambda j: ag_from(j).wait_recv())
            adapt(i)
            places(i * GROUP, (i + 1) * GROUP, lambda k: ret_to(k).start())


    def gradients(i):
        got = disp_recv[pl.ds(i * GROUP, GROUP)].reshape(GROUP * 2 * chunk, hs + hw)
        low, back = by_slot(ranked(i), got_tags(i))
        low = low.reshape(GROUP, chunk, 128)
        back = back.reshape(GROUP, chunk, 128)
        zero = jnp.zeros_like(low)

        def part(value, h, rows_of):
            pair = [value, zero] if h == 0 else [zero, value]
            wide = jnp.concatenate(pair, axis=1).reshape(GROUP * 2 * chunk, 128).astype(bf16)
            return lax.dot_general(wide, rows_of, contract_first, preferred_element_type=f32)

        for h in range(2):
            gd_ref[:, h * hs:(h + 1) * hs] += part(back, h, got[:, :hs])
            gu_ref[:, h * hw:(h + 1) * hw] += part(low, h, got[:, hs:])

    def ret_arrive(half):
        @pl.loop(half * groups, (half + 1) * groups)
        def _(i):
            arrived(i, ret_recv, ret_ssem, ret_rsem)
            take(i)

    scatter(0)
    reduce(0)
    gd_ref[...] = jnp.zeros_like(gd_ref)
    gu_ref[...] = jnp.zeros_like(gu_ref)
    scatter(1)
    give_back(0)
    reduce(1)
    several(part_recv, n_f - 1, part_ssem, part_rsem).wait_recv()
    acc[...] = part_recv[0].astype(f32)

    @pl.loop(1, n_f)
    def _(j):
        acc[...] += part_recv[j].astype(f32)

    pl.loop(0, groups)(gradients)
    give_back(1)
    ret_recv[pl.ds(last, 1)] = ret_send[pl.ds(last, 1)]
    pl.loop(groups, 2 * groups)(gradients)

    for load in loads[7:]:
        load.wait()
    for maps, rate, grad, mean, square, new_mean, new_square in (
        (d_ref, rate_down, gd_ref, md_ref, sd_ref, md_out, sd_out),
        (u_ref, rate_up, gu_ref, mu_ref, su_ref, mu_out, su_out),
    ):
        theta = maps[...].astype(f32) - (rate * adapter_scale) * grad[...]
        new_mean[...] = (SNAPS * mean[...] + theta) / (SNAPS + 1.0)
        new_square[...] = (SNAPS * square[...] + theta * theta) / (SNAPS + 1.0)

    ret_arrive(0)
    ret_arrive(1)
    out_ref[...] = acc[...].astype(bf16)

    dp_copy(
        wt_all.at[pl.ds(0, half_z), 0], wt_all.at[pl.ds(0, half_z), 0], ring_r_send, ring_r_recv.at[0], right
    ).wait_send()
    dp_copy(
        wt_all.at[pl.ds(0, half_z - 1), 0], wt_all.at[pl.ds(0, half_z - 1), 0], ring_l_send, ring_l_recv.at[0], left
    ).wait_send()
    dp_copy(wt_all.at[:, 0], wt_all.at[:, 0], sib_send, sib_recv.at[0], sibling).wait_send()
    several(disp_send, n_dp - 1, disp_ssem, disp_rsem.at[0]).wait_send()
    several(part_send, n_f - 1, part_ssem, part_rsem).wait_send()
    several(lr_send, n_f - 1, rs_ssem, rs_rsem).wait_send()
    several(lr_all, n_f - 1, ag_ssem, ag_rsem.at[0]).wait_send()
    several(ret_send, n_dp - 1, ret_ssem, ret_rsem.at[0]).wait_send()


def fused(x, g, w, down, up, block_member, member_slot, *moments):
    n_dp, n_f = lax.axis_size("dp"), lax.axis_size("fsdp")
    rows, slab = x.shape
    width = g.shape[1]
    cap = 2 * block_member.shape[1] // n_dp
    chunk = cap * BLK
    n_z = n_dp // 2
    vmem = pl.BlockSpec(memory_space=pltpu.VMEM)
    hbm = pl.BlockSpec(memory_space=pltpu.HBM)
    dma = pltpu.SemaphoreType.DMA
    hops = (n_z // 2 + 1) * PIECES
    return pl.pallas_call(
        functools.partial(kernel, (n_dp, n_f, cap)),
        out_shape=(
            jax.ShapeDtypeStruct((rows, width), bf16),
        )
        + tuple(jax.ShapeDtypeStruct(moment.shape, f32) for moment in moments),
        in_specs=[hbm] * 11,
        out_specs=(vmem,) * 5,
        scratch_shapes=[
            pltpu.VMEM(x.shape, bf16), pltpu.VMEM(g.shape, bf16),
            pltpu.VMEM(down.shape, bf16), pltpu.VMEM(up.shape, bf16),
            pltpu.VMEM(block_member.shape, jnp.int32), pltpu.VMEM(member_slot.shape, jnp.int32),
            *(pltpu.VMEM(moment.shape, f32) for moment in moments),
            pltpu.VMEM(down.shape, f32), pltpu.VMEM(up.shape, f32),
            pltpu.VMEM((n_z, 2, w.shape[0] + 16, 128), bf16),
            pltpu.VMEM((n_dp, 2 * chunk, (slab + width) // 2), bf16),
            pltpu.VMEM((n_dp, 2 * chunk, (slab + width) // 2), bf16),
            pltpu.VMEM((n_f, rows, width), bf16),
            pltpu.VMEM((n_f, rows, width), bf16),
            pltpu.VMEM((n_f, 2 * chunk, 128), bf16),
            pltpu.VMEM((n_f, 2 * chunk, 128), bf16),
            pltpu.VMEM((n_f, 2 * chunk, 128), bf16),
            pltpu.VMEM((n_dp, 2 * chunk, width // 2), bf16),
            pltpu.VMEM((n_dp, 2 * chunk, width // 2), bf16),
            pltpu.VMEM((rows, width), f32),
            dma((11,)), dma, dma((hops,)), dma, dma((hops,)), dma, dma((n_z,)),
            dma, dma((n_dp // GROUP,)), dma, dma, dma, dma, dma, dma((n_f,)), dma, dma((n_dp // GROUP,)),
        ],
        compiler_params=pltpu.CompilerParams(
            collective_id=0, has_side_effects=True, vmem_limit_bytes=60 * 1024 * 1024
        ),
        name="adapter_step",
    )(x, g, w, down, up, block_member, member_slot, *moments)


def settle(*results):
    n = len(results)

    def move(*refs):
        here, sems = refs[2 * n:3 * n], refs[-1]
        loads = [pltpu.make_async_copy(refs[i], here[i], sems.at[i]) for i in range(n)]
        stores = [pltpu.make_async_copy(here[i], refs[n + i], sems.at[n + i]) for i in range(n)]
        for load in loads:
            load.start()
        for load, store in zip(loads, stores):
            load.wait()
            store.start()
        for store in stores:
            store.wait()

    anywhere = pl.BlockSpec(memory_space=pl.ANY)
    return pl.pallas_call(
        move,
        out_shape=tuple(jax.ShapeDtypeStruct(r.shape, r.dtype) for r in results),
        in_specs=[anywhere] * n,
        out_specs=(anywhere,) * n,
        scratch_shapes=[*(pltpu.VMEM(r.shape, r.dtype) for r in results), pltpu.SemaphoreType.DMA((2 * n,))],
        name="settle",
    )(*results)


def body(
    inputs, out_grad, base_weight, down_maps, up_maps,
    mean_down, square_down, mean_up, square_up, block_member, member_slot,
):
    maps = (down_maps, up_maps)
    moments = (mean_down, square_down, mean_up, square_up)

    def flat(value):
        return value.reshape(-1, value.shape[2])

    projected, *news = settle(
        *fused(
            inputs, out_grad, base_weight, *map(flat, maps),
            block_member.reshape(1, -1), member_slot.reshape(1, -1), *map(flat, moments),
        )
    )
    return (projected, *(new.reshape(old.shape) for new, old in zip(news, moments)))


def solution(mesh):
    split = P("dp", None, "fsdp")
    placed = (P("dp", "fsdp"), P("dp", "fsdp"), P("fsdp", "dp")) + (split,) * 6 + (P("dp"), P())
    return jax.shard_map(
        body,
        mesh=mesh,
        in_specs=placed,
        out_specs=(P("dp", "fsdp"),) + (split,) * 4,
        check_vma=False,
    )
```
